512 devices in a mesh: dp: 64 (over z_lo, y, core), fsdp: 8 (over x, z_hi).
Axes of the slice: x: 4, y: 4, z: 16 (z_hi: 2, z_lo: 8; z = z_hi * 8 + z_lo), core: 2. Of those that a mesh axis runs over, the one named last changes fastest.
Arguments:
- tokens: bfloat16 [512, 16384], P('dp', 'fsdp'), may hold values from -6 to 6
- route_plan: int32 [4], replicated, may hold values from -1 to 3, as said below
- block_tokens: int32 [4], replicated, may hold values from 1 to 128
- gate_up: bfloat16 [16384, 2, 26624], P('fsdp', None, 'dp'), may hold values from -0.046875 to 0.046875
- down_proj: bfloat16 [26624, 16384], P('dp', 'fsdp'), may hold values from -0.0390625 to 0.0390625
Outputs:
- layer_output: bfloat16 [512, 16384], P('dp', 'fsdp')
The draws below stay inside these ranges and needn't reach their ends.
Inputs may be any that keep to these rules, and one draw needn't show every extreme that they name: route_plan[b] is -1 for an empty source block; no two source blocks name the same destination block.
All inputs are finite; a program needn't handle non-finite values.
Results may differ from the reference program's by a relative error of at most 0.0049.
Values may be sent and summed in bfloat16 or wider, within the bound.
No kernel may reach another device: no remote copies, remote signals or barrier semaphores. Data moves between devices by JAX's collectives and lax.ppermute only.
A program may use at most 64 MiB of HBM per device.

```python
import jax
import jax.numpy as jnp
from jax import lax

D = 16384
HB = 26624
BLK = 128
ROWS = 512
BLOCKS = 4


def draw_route_plan(key, part):
    key = jax.random.fold_in(key, 11)
    order_key, flag_key, pick_key = jax.random.split(key, 3)
    scores = jax.random.randint(order_key, (BLOCKS,), 0, 1 << 20) * BLOCKS + jnp.arange(BLOCKS, dtype=jnp.int32)
    mapping = jnp.argsort(scores).astype(jnp.int32)
    flags = jax.random.randint(flag_key, (BLOCKS,), 0, 4)
    empty_target = jax.random.randint(pick_key, (), 0, BLOCKS - 1)
    dropped = (flags == 0) | (mapping == empty_target)
    dropped = dropped & (mapping != BLOCKS - 1)
    return jnp.where(dropped, -1, mapping).astype(jnp.int32)


def draw_block_tokens(key, part):
    key = jax.random.fold_in(key, 23)
    short_key, flag_key, pick_key = jax.random.split(key, 3)
    short_count = jax.random.randint(short_key, (BLOCKS,), 1, BLK + 1)
    full_flag = jax.random.randint(flag_key, (BLOCKS,), 0, 4)
    token_count = jnp.where(full_flag > 0, BLK, short_count)
    short_block = jax.random.randint(pick_key, (), 0, BLOCKS)
    token_count = token_count.at[short_block].set(1)
    token_count = token_count.at[(short_block + 1) % BLOCKS].set(BLK)
    return token_count.astype(jnp.int32)


def steps_of(rng, extent, cuts, low, largest):
    def one(position, parts):
        draws = jax.random.uniform(jax.random.fold_in(jax.random.fold_in(rng, 6), position), (parts,), jnp.float32, low / len(cuts), largest / len(cuts))
        return jnp.repeat(jnp.exp(draws), extent[position] // parts).reshape((-1,) + (1,) * (len(extent) - position - 1))

    factor_of = one(*cuts[0])
    for cut in cuts[1:]:
        factor_of = factor_of * one(*cut)
    return factor_of


def noise(own_key, shape, deviation, reach, cuts=(), held_as=jnp.bfloat16):
    factor_of = steps_of(own_key, shape, cuts, -0.22, 0.18) if cuts else 1.0
    entries = jax.random.normal(own_key, shape, jnp.float32) * deviation * factor_of
    return jnp.minimum(jnp.maximum(entries, -reach), reach).astype(held_as)


def setup_inputs(seed: int = 0) -> dict:
    keys = jax.random.split(jax.random.key(seed), 6)
    tokens = noise(keys[0], (ROWS, D), 1.0, 6.0, ((0, 64), (1, 8)))
    route_plan = draw_route_plan(jax.random.fold_in(keys[5], 71), 0)
    block_tokens = draw_block_tokens(jax.random.fold_in(keys[5], 71), 0)
    gate_up = noise(keys[3], (D, 2, HB), D ** -0.5, 0.046875, ((0, 8), (2, 64)))
    down_proj = noise(keys[4], (HB, D), HB ** -0.5, 0.0390625, ((0, 64), (1, 8)))
    return dict(tokens=tokens, route_plan=route_plan, block_tokens=block_tokens, gate_up=gate_up, down_proj=down_proj)


def reference(tokens, route_plan, block_tokens, gate_up, down_proj):
    live_rows = lax.broadcasted_iota(jnp.int32, (BLOCKS, BLK), 1) < block_tokens[:, None]
    masked = jnp.where(live_rows.reshape(ROWS, 1), tokens, jnp.zeros_like(tokens))
    gate = jnp.dot(masked, gate_up[:, 0, :], preferred_element_type=jnp.float32)
    up = jnp.dot(masked, gate_up[:, 1, :], preferred_element_type=jnp.float32)
    hidden = (jax.nn.silu(gate) * up).astype(jnp.bfloat16)
    destination = jnp.where(route_plan >= 0, route_plan, BLOCKS).astype(jnp.int32)
    source = jnp.full((BLOCKS + 1,), -1, jnp.int32).at[destination].set(jnp.arange(BLOCKS, dtype=jnp.int32))[:BLOCKS]
    blocks = hidden.reshape(BLOCKS, BLK * HB)
    picked = blocks[jnp.maximum(source, 0)]
    delivered = jnp.where((source >= 0)[:, None], picked, jnp.zeros_like(picked))
    return jnp.dot(delivered.reshape(ROWS, HB), down_proj, preferred_element_type=jnp.float32).astype(jnp.bfloat16)
```

```python
import functools

import jax
import jax.numpy as jnp
from jax import lax
from jax.experimental import pallas as pl
from jax.experimental.pallas import tpu as pltpu
from jax.sharding import Mesh
from jax.sharding import PartitionSpec as P

BLK = 128
HALF = 64
ZL, YY, CC, XX, ZH = 8, 4, 2, 4, 2
SIZES = (8,)
BF16, F32 = jnp.bfloat16, jnp.float32


def halves_of(plan, lives):
    slot = jnp.int32(0)
    for h in range(ZL):
        block, part = h // 2, h % 2
        live = (plan(block) >= 0) & (lives(block) > HALF * part)
        yield h, block, part, live, slot
        slot = slot + live.astype(jnp.int32)


def pack_kernel(slots, plan_ref, lives_ref, place_ref, rows_ref, out_ref):
    row = lax.broadcasted_iota(jnp.int32, rows_ref.shape[1:], 0) + place_ref[0]
    count = jnp.int32(0)
    for h, block, part, live, slot in halves_of(lambda b: plan_ref[b], lambda b: lives_ref[b]):
        count = slot + live.astype(jnp.int32)

        @pl.when(live)
        def _():
            kept = row + HALF * part < lives_ref[block]
            rows = jnp.where(kept, rows_ref[h].astype(F32), 0.0).astype(BF16)
            for copy in range(YY):
                out_ref[copy, slot] = rows

    for s in range(slots):

        @pl.when(s >= count)
        def _():
            for copy in range(YY):
                out_ref[copy, s] = jnp.zeros(out_ref.shape[2:], BF16)


def place_kernel(plan_ref, lives_ref, parts_ref, out_ref):
    out_ref[...] = jnp.zeros(out_ref.shape, BF16)
    for h, block, part, live, slot in halves_of(lambda b: plan_ref[b], lambda b: lives_ref[b]):

        @pl.when(live)
        def _():
            total = parts_ref[0, slot].astype(F32)
            for k in range(1, YY):
                total = total + parts_ref[k, slot].astype(F32)
            out_ref[2 * plan_ref[block] + part] = total.astype(BF16)


def local_call(kernel, scalars, shape):
    return pl.pallas_call(
        kernel,
        out_shape=jax.ShapeDtypeStruct(shape, BF16),
        in_specs=[pl.BlockSpec(memory_space=pltpu.SMEM)] * scalars + [pl.BlockSpec(memory_space=pltpu.VMEM)],
        out_specs=pl.BlockSpec(memory_space=pltpu.VMEM),
        compiler_params=pltpu.CompilerParams(vmem_limit_bytes=16 << 20),
    )


def exchange(array, axis):
    return lax.all_to_all(array, axis, 0, 0, tiled=False)


def swap(array, axis):
    return lax.ppermute(array, axis, [(0, 1), (1, 0)])


def spread(array, copies):
    return jnp.broadcast_to(array[None], (copies,) + array.shape)


def block_rows(slots, gathered, plan, lives, weights, down):
    features, hidden = weights.shape[0], down.shape[0]
    per = slots * 8
    place = (lax.axis_index("y") * 16 + lax.axis_index("c") * 8).reshape(1)
    packed = local_call(functools.partial(pack_kernel, slots), 3, (YY, slots, 8, features))(plan, lives, place, gathered)
    mine = exchange(packed.reshape(YY, per, features), "y").reshape(YY * per, features)
    rows = jnp.concatenate([mine, swap(mine, "c")], axis=0)
    total = rows.shape[0]

    share = hidden // XX
    partial = lax.dot_general(
        weights.transpose(1, 2, 0).reshape(2 * hidden, features), rows, (((1,), (1,)), ((), ())), preferred_element_type=F32
    )
    partial = partial.reshape(2, XX, share, total).transpose(1, 0, 2, 3)
    along_x = jnp.sum(exchange(partial, "x"), axis=0)
    other = swap(along_x.astype(BF16), "zh").astype(F32)
    summed = along_x + other
    act = (jax.nn.silu(summed[0]) * summed[1]).astype(BF16)
    act = exchange(spread(act, XX), "x").reshape(hidden, total)

    def project(part):
        return lax.dot_general(part, down, (((0,), (0,)), ((), ())), preferred_element_type=F32)

    theirs = swap(project(act[:, total // 2 :]), "c")
    ours = (project(act[:, : total // 2]) + theirs).astype(BF16)
    parts = exchange(ours.reshape(YY, per, -1), "y").reshape(YY, slots, 8, -1)
    return local_call(place_kernel, 2, (ZL, 8, down.shape[1]))(plan, lives, parts)


def body(tokens, plan, lives, weights, down):
    gathered = exchange(spread(tokens, ZL), "zl")
    if len(SIZES) == 1:
        placed = block_rows(SIZES[0], gathered, plan, lives, weights, down)
    else:
        count = jnp.sum((plan >= 0) * (1 + (lives > HALF)))
        which = sum((count > n).astype(jnp.int32) for n in SIZES[:-1])
        placed = lax.switch(
            which, [functools.partial(block_rows, n) for n in SIZES], gathered, plan, lives, weights, down
        )
    sums = exchange(placed, "zl")
    total = sums[0].astype(F32)
    for k in range(1, ZL):
        total = total + sums[k].astype(F32)
    return total.astype(BF16)


def solution(mesh):
    fine = Mesh(mesh.devices.reshape(ZL, YY, CC, XX, ZH), ("zl", "y", "c", "x", "zh"))
    dp, fsdp = ("zl", "y", "c"), ("x", "zh")
    return jax.shard_map(
        body,
        mesh=fine,
        in_specs=(P(dp, fsdp), P(), P(), P(fsdp, None, dp), P(dp, fsdp)),
        out_specs=P(dp, fsdp),
        check_vma=False,
    )
```

```python
import functools

import jax
import jax.numpy as jnp
from jax import lax
from jax.experimental import pallas as pl
from jax.experimental.pallas import tpu as pltpu
from jax.sharding import Mesh
from jax.sharding import PartitionSpec as P

BLK = 128
HALF = 64
ZL, YY, CC, XX, ZH = 8, 4, 2, 4, 2
SIZES = (2, 4, 6, 8)
BF16, F32 = jnp.bfloat16, jnp.float32


def halves_of(plan, lives):
    slot = jnp.int32(0)
    for h in range(ZL):
        block, part = h // 2, h % 2
        live = (plan(block) >= 0) & (lives(block) > HALF * part)
        yield h, block, part, live, slot
        slot = slot + live.astype(jnp.int32)


def pack_kernel(slots, plan_ref, lives_ref, place_ref, rows_ref, out_ref):
    row = lax.broadcasted_iota(jnp.int32, rows_ref.shape[1:], 0) + place_ref[0]
    count = jnp.int32(0)
    for h, block, part, live, slot in halves_of(lambda b: plan_ref[b], lambda b: lives_ref[b]):
        count = slot + live.astype(jnp.int32)

        @pl.when(live)
        def _():
            kept = row + HALF * part < lives_ref[block]
            rows = jnp.where(kept, rows_ref[h].astype(F32), 0.0).astype(BF16)
            for copy in range(YY):
                out_ref[copy, slot] = rows

    for s in range(slots):

        @pl.when(s >= count)
        def _():
            for copy in range(YY):
                out_ref[copy, s] = jnp.zeros(out_ref.shape[2:], BF16)


def place_kernel(plan_ref, lives_ref, parts_ref, out_ref):
    out_ref[...] = jnp.zeros(out_ref.shape, BF16)
    for h, block, part, live, slot in halves_of(lambda b: plan_ref[b], lambda b: lives_ref[b]):

        @pl.when(live)
        def _():
            total = parts_ref[0, slot].astype(F32)
            for k in range(1, YY):
                total = total + parts_ref[k, slot].astype(F32)
            out_ref[2 * plan_ref[block] + part] = total.astype(BF16)


def local_call(kernel, scalars, shape):
    return pl.pallas_call(
        kernel,
        out_shape=jax.ShapeDtypeStruct(shape, BF16),
        in_specs=[pl.BlockSpec(memory_space=pltpu.SMEM)] * scalars + [pl.BlockSpec(memory_space=pltpu.VMEM)],
        out_specs=pl.BlockSpec(memory_space=pltpu.VMEM),
        compiler_params=pltpu.CompilerParams(vmem_limit_bytes=16 << 20),
    )


def exchange(array, axis):
    return lax.all_to_all(array, axis, 0, 0, tiled=False)


def swap(array, axis):
    return lax.ppermute(array, axis, [(0, 1), (1, 0)])


def spread(array, copies):
    return jnp.broadcast_to(array[None], (copies,) + array.shape)


def block_rows(slots, gathered, plan, lives, weights, down):
    features, hidden = weights.shape[0], down.shape[0]
    per = slots * 8
    place = (lax.axis_index("y") * 16 + lax.axis_index("c") * 8).reshape(1)
    packed = local_call(functools.partial(pack_kernel, slots), 3, (YY, slots, 8, features))(plan, lives, place, gathered)
    mine = exchange(packed.reshape(YY, per, features), "y").reshape(YY * per, features)
    rows = jnp.concatenate([mine, swap(mine, "c")], axis=0)
    total = rows.shape[0]

    share = hidden // XX
    partial = lax.dot_general(
        weights.transpose(1, 2, 0).reshape(2 * hidden, features), rows, (((1,), (1,)), ((), ())), preferred_element_type=F32
    )
    partial = partial.reshape(2, XX, share, total).transpose(1, 0, 2, 3)
    along_x = jnp.sum(exchange(partial, "x"), axis=0)
    other = swap(along_x.astype(BF16), "zh").astype(F32)
    summed = along_x + other
    act = (jax.nn.silu(summed[0]) * summed[1]).astype(BF16)
    act = exchange(spread(act, XX), "x").reshape(hidden, total)

    def project(part):
        return lax.dot_general(part, down, (((0,), (0,)), ((), ())), preferred_element_type=F32)

    theirs = swap(project(act[:, total // 2 :]), "c")
    ours = (project(act[:, : total // 2]) + theirs).astype(BF16)
    parts = exchange(ours.reshape(YY, per, -1), "y").reshape(YY, slots, 8, -1)
    return local_call(place_kernel, 2, (ZL, 8, down.shape[1]))(plan, lives, parts)


def body(tokens, plan, lives, weights, down):
    gathered = exchange(spread(tokens, ZL), "zl")
    if len(SIZES) == 1:
        placed = block_rows(SIZES[0], gathered, plan, lives, weights, down)
    else:
        count = jnp.sum((plan >= 0) * (1 + (lives > HALF)))
        which = sum((count > n).astype(jnp.int32) for n in SIZES[:-1])
        placed = lax.switch(
            which, [functools.partial(block_rows, n) for n in SIZES], gathered, plan, lives, weights, down
        )
    sums = exchange(placed, "zl")
    total = sums[0].astype(F32)
    for k in range(1, ZL):
        total = total + sums[k].astype(F32)
    return total.astype(BF16)


def solution(mesh):
    fine = Mesh(mesh.devices.reshape(ZL, YY, CC, XX, ZH), ("zl", "y", "c", "x", "zh"))
    dp, fsdp = ("zl", "y", "c"), ("x", "zh")
    return jax.shard_map(
        body,
        mesh=fine,
        in_specs=(P(dp, fsdp), P(), P(), P(fsdp, None, dp), P(dp, fsdp)),
        out_specs=P(dp, fsdp),
        check_vma=False,
    )
```

```python
import functools

import jax
import jax.numpy as jnp
from jax import lax
from jax.experimental import pallas as pl
from jax.experimental.pallas import tpu as pltpu
from jax.sharding import Mesh
from jax.sharding import PartitionSpec as P

BLK = 128
HALF = 64
ZL, YY, CC, XX, ZH = 8, 4, 2, 4, 2
SIZES = (2, 3, 4, 5, 6, 8)
BF16, F32 = jnp.bfloat16, jnp.float32


def halves_of(plan, lives):
    slot = jnp.int32(0)
    for h in range(ZL):
        block, part = h // 2, h % 2
        live = (plan(block) >= 0) & (lives(block) > HALF * part)
        yield h, block, part, live, slot
        slot = slot + live.astype(jnp.int32)


def pack_kernel(slots, plan_ref, lives_ref, place_ref, rows_ref, out_ref):
    row = lax.broadcasted_iota(jnp.int32, rows_ref.shape[1:], 0) + place_ref[0]
    count = jnp.int32(0)
    for h, block, part, live, slot in halves_of(lambda b: plan_ref[b], lambda b: lives_ref[b]):
        count = slot + live.astype(jnp.int32)

        @pl.when(live)
        def _():
            kept = row + HALF * part < lives_ref[block]
            rows = jnp.where(kept, rows_ref[h].astype(F32), 0.0).astype(BF16)
            for copy in range(YY):
                out_ref[copy, slot] = rows

    for s in range(slots):

        @pl.when(s >= count)
        def _():
            for copy in range(YY):
                out_ref[copy, s] = jnp.zeros(out_ref.shape[2:], BF16)


def place_kernel(plan_ref, lives_ref, parts_ref, out_ref):
    out_ref[...] = jnp.zeros(out_ref.shape, BF16)
    for h, block, part, live, slot in halves_of(lambda b: plan_ref[b], lambda b: lives_ref[b]):

        @pl.when(live)
        def _():
            total = parts_ref[0, slot].astype(F32)
            for k in range(1, YY):
                total = total + parts_ref[k, slot].astype(F32)
            out_ref[2 * plan_ref[block] + part] = total.astype(BF16)


def local_call(kernel, scalars, shape):
    return pl.pallas_call(
        kernel,
        out_shape=jax.ShapeDtypeStruct(shape, BF16),
        in_specs=[pl.BlockSpec(memory_space=pltpu.SMEM)] * scalars + [pl.BlockSpec(memory_space=pltpu.VMEM)],
        out_specs=pl.BlockSpec(memory_space=pltpu.VMEM),
        compiler_params=pltpu.CompilerParams(vmem_limit_bytes=16 << 20),
    )


def exchange(array, axis):
    return lax.all_to_all(array, axis, 0, 0, tiled=False)


def swap(array, axis):
    return lax.ppermute(array, axis, [(0, 1), (1, 0)])


def spread(array, copies):
    return jnp.broadcast_to(array[None], (copies,) + array.shape)


def block_rows(slots, gathered, plan, lives, weights, down):
    features, hidden = weights.shape[2], down.shape[0]
    per = slots * 8
    place = (lax.axis_index("y") * 16 + lax.axis_index("c") * 8).reshape(1)
    packed = local_call(functools.partial(pack_kernel, slots), 3, (YY, slots, 8, features))(plan, lives, place, gathered)
    rows = exchange(packed.reshape(YY, per, features), "y").reshape(YY * per, features)

    partial = lax.dot_general(
        rows, weights.reshape(2 * hidden, features), (((1,), (1,)), ((), ())), preferred_element_type=F32
    )
    along_x = jnp.sum(exchange(partial.reshape(XX, per, 2 * hidden), "x"), axis=0)
    other = swap(along_x.astype(BF16), "zh").astype(F32)
    summed = along_x + other
    act = (jax.nn.silu(summed[:, :hidden]) * summed[:, hidden:]).astype(BF16)
    act = exchange(spread(act, XX), "x").reshape(XX * per, hidden)

    ours = jnp.dot(act, down, preferred_element_type=F32).astype(BF16)
    parts = exchange(ours.reshape(YY, per, -1), "y").reshape(YY, slots, 8, -1)
    return local_call(place_kernel, 2, (ZL, 8, down.shape[1]))(plan, lives, parts)


def body(tokens, plan, lives, weights, down):
    gathered = exchange(spread(tokens, ZL), "zl")
    weights = weights.transpose(1, 2, 0)
    weights = jnp.concatenate([weights, swap(weights, "c")], axis=1)
    down = jnp.concatenate([down, swap(down, "c")], axis=0)
    if len(SIZES) == 1:
        placed = block_rows(SIZES[0], gathered, plan, lives, weights, down)
    else:
        count = jnp.sum((plan >= 0) * (1 + (lives > HALF)))
        which = sum((count > n).astype(jnp.int32) for n in SIZES[:-1])
        placed = lax.switch(
            which, [functools.partial(block_rows, n) for n in SIZES], gathered, plan, lives, weights, down
        )
    sums = exchange(placed, "zl")
    total = sums[0].astype(F32)
    for k in range(1, ZL):
        total = total + sums[k].astype(F32)
    return total.astype(BF16)


def solution(mesh):
    fine = Mesh(mesh.devices.reshape(ZL, YY, CC, XX, ZH), ("zl", "y", "c", "x", "zh"))
    dp, fsdp = ("zl", "y", "c"), ("x", "zh")
    return jax.shard_map(
        body,
        mesh=fine,
        in_specs=(P(dp, fsdp), P(), P(), P(fsdp, None, dp), P(dp, fsdp)),
        out_specs=P(dp, fsdp),
        check_vma=False,
    )
```

```python
import functools

import jax
import jax.numpy as jnp
from jax import lax
from jax.experimental import pallas as pl
from jax.experimental.pallas import tpu as pltpu
from jax.sharding import Mesh
from jax.sharding import PartitionSpec as P

BLK = 128
HALF = 64
ZL, YY, CC, XX, ZH = 8, 4, 2, 4, 2
WIDE = 256
SIZES = (2, 3, 4, 5, 6, 8)
BF16, F32 = jnp.bfloat16, jnp.float32


def halves_of(plan, lives):
    slot = jnp.int32(0)
    for h in range(ZL):
        block, part = h // 2, h % 2
        live = (plan(block) >= 0) & (lives(block) > HALF * part)
        yield h, block, part, live, slot
        slot = slot + live.astype(jnp.int32)


def pack_kernel(slots, plan_ref, lives_ref, place_ref, rows_ref, out_ref):
    row = lax.broadcasted_iota(jnp.int32, rows_ref.shape[1:], 0) + place_ref[0]
    count = jnp.int32(0)
    for h, block, part, live, slot in halves_of(lambda b: plan_ref[b], lambda b: lives_ref[b]):
        count = slot + live.astype(jnp.int32)

        @pl.when(live)
        def _():
            kept = row + HALF * part < lives_ref[block]
            rows = jnp.where(kept, rows_ref[h].astype(F32), 0.0).astype(BF16)
            for copy in range(YY):
                out_ref[copy, slot] = rows

    for s in range(slots):

        @pl.when(s >= count)
        def _():
            for copy in range(YY):
                out_ref[copy, s] = jnp.zeros(out_ref.shape[2:], BF16)


def place_kernel(plan_ref, lives_ref, parts_ref, out_ref):
    out_ref[...] = jnp.zeros(out_ref.shape, BF16)
    for h, block, part, live, slot in halves_of(lambda b: plan_ref[b], lambda b: lives_ref[b]):

        @pl.when(live)
        def _():
            total = parts_ref[0, slot].astype(F32)
            for k in range(1, YY):
                total = total + parts_ref[k, slot].astype(F32)
            out_ref[2 * plan_ref[block] + part] = total.astype(BF16)


def project_kernel(rows_ref, own_ref, other_ref, out_ref, weights, arrived):
    share = own_ref.shape[1]
    copies = []
    for k in range(4):
        source = (own_ref, other_ref)[k % 2]
        copies.append(
            pltpu.make_async_copy(source.at[k // 2], weights.at[pl.ds(k * share, share)], arrived.at[k])
        )
        copies[-1].start()
    rows = rows_ref[...]
    have = 0
    for low in range(0, 4 * share, WIDE):
        high = min(low + WIDE, 4 * share)
        while have < high:
            copies[have // share].wait()
            have += share
        out_ref[:, low:high] = lax.dot_general(
            rows, weights[low:high], (((1,), (1,)), ((), ())), preferred_element_type=F32
        )


def project(rows, own, other):
    count, features = rows.shape
    columns = 4 * own.shape[1]
    return pl.pallas_call(
        project_kernel,
        out_shape=jax.ShapeDtypeStruct((count, columns), F32),
        in_specs=[pl.BlockSpec(memory_space=pltpu.VMEM)] + [pl.BlockSpec(memory_space=pl.ANY)] * 2,
        out_specs=pl.BlockSpec(memory_space=pltpu.VMEM),
        scratch_shapes=[pltpu.VMEM((columns, features), BF16), pltpu.SemaphoreType.DMA((4,))],
        compiler_params=pltpu.CompilerParams(vmem_limit_bytes=32 << 20),
        cost_estimate=pl.CostEstimate(
            flops=2 * count * columns * features, bytes_accessed=2 * columns * features, transcendentals=0
        ),
    )(rows, own, other)


def local_call(kernel, scalars, shape):
    return pl.pallas_call(
        kernel,
        out_shape=jax.ShapeDtypeStruct(shape, BF16),
        in_specs=[pl.BlockSpec(memory_space=pltpu.SMEM)] * scalars + [pl.BlockSpec(memory_space=pltpu.VMEM)],
        out_specs=pl.BlockSpec(memory_space=pltpu.VMEM),
        compiler_params=pltpu.CompilerParams(vmem_limit_bytes=16 << 20),
    )


def exchange(array, axis):
    return lax.all_to_all(array, axis, 0, 0, tiled=False)


def swap(array, axis):
    return lax.ppermute(array, axis, [(0, 1), (1, 0)])


def spread(array, copies):
    return jnp.broadcast_to(array[None], (copies,) + array.shape)


def block_rows(slots, gathered, plan, lives, own, other, down):
    features, hidden = own.shape[2], 2 * down.shape[0]
    per = slots * 8
    place = (lax.axis_index("y") * 16 + lax.axis_index("c") * 8).reshape(1)
    packed = local_call(functools.partial(pack_kernel, slots), 3, (YY, slots, 8, features))(plan, lives, place, gathered)
    rows = exchange(packed.reshape(YY, per, features), "y").reshape(YY * per, features)

    partial = project(rows, own, other)
    along_x = jnp.sum(exchange(partial.reshape(XX, per, 2 * hidden), "x"), axis=0)
    along_x, down = lax.optimization_barrier((along_x, down))
    across = swap(along_x.astype(BF16), "zh").astype(F32)
    down = jnp.concatenate([down, swap(down, "c")], axis=0)
    summed = along_x + across
    act = (jax.nn.silu(summed[:, :hidden]) * summed[:, hidden:]).astype(BF16)
    act = exchange(spread(act, XX), "x").reshape(XX * per, hidden)

    ours = jnp.dot(act, down, preferred_element_type=F32).astype(BF16)
    parts = exchange(ours.reshape(YY, per, -1), "y").reshape(YY, slots, 8, -1)
    return local_call(place_kernel, 2, (ZL, 8, down.shape[1]))(plan, lives, parts)


def body(tokens, plan, lives, weights, down):
    gathered = exchange(spread(tokens, ZL), "zl")
    weights = weights.transpose(1, 2, 0)
    other = swap(weights, "c")
    if len(SIZES) == 1:
        placed = block_rows(SIZES[0], gathered, plan, lives, weights, other, down)
    else:
        count = jnp.sum((plan >= 0) * (1 + (lives > HALF)))
        which = sum((count > n).astype(jnp.int32) for n in SIZES[:-1])
        placed = lax.switch(
            which, [functools.partial(block_rows, n) for n in SIZES], gathered, plan, lives, weights, other, down
        )
    sums = exchange(placed, "zl")
    total = sums[0].astype(F32)
    for k in range(1, ZL):
        total = total + sums[k].astype(F32)
    return total.astype(BF16)


def solution(mesh):
    fine = Mesh(mesh.devices.reshape(ZL, YY, CC, XX, ZH), ("zl", "y", "c", "x", "zh"))
    dp, fsdp = ("zl", "y", "c"), ("x", "zh")
    return jax.shard_map(
        body,
        mesh=fine,
        in_specs=(P(dp, fsdp), P(), P(), P(fsdp, None, dp), P(dp, fsdp)),
        out_specs=P(dp, fsdp),
        check_vma=False,
    )
```

```python
import functools

import jax
import jax.numpy as jnp
from jax import lax
from jax.experimental import pallas as pl
from jax.experimental.pallas import tpu as pltpu
from jax.sharding import Mesh
from jax.sharding import PartitionSpec as P

BLK = 128
HALF = 64
ZL, YY, CC, XX, ZH = 8, 4, 2, 4, 2
WIDE = 256
SIZES = (2, 3, 4, 5, 6, 8)
BF16, F32 = jnp.bfloat16, jnp.float32


def halves_of(plan, lives):
    slot = jnp.int32(0)
    for h in range(ZL):
        block, part = h // 2, h % 2
        live = (plan(block) >= 0) & (lives(block) > HALF * part)
        yield h, block, part, live, slot
        slot = slot + live.astype(jnp.int32)


def pack_kernel(slots, plan_ref, lives_ref, place_ref, rows_ref, out_ref):
    row = lax.broadcasted_iota(jnp.int32, rows_ref.shape[1:], 0) + place_ref[0]
    count = jnp.int32(0)
    for h, block, part, live, slot in halves_of(lambda b: plan_ref[b], lambda b: lives_ref[b]):
        count = slot + live.astype(jnp.int32)

        @pl.when(live)
        def _():
            kept = row + HALF * part < lives_ref[block]
            rows = jnp.where(kept, rows_ref[h].astype(F32), 0.0).astype(BF16)
            for copy in range(YY):
                out_ref[copy, slot] = rows

    for s in range(slots):

        @pl.when(s >= count)
        def _():
            for copy in range(YY):
                out_ref[copy, s] = jnp.zeros(out_ref.shape[2:], BF16)


def place_kernel(plan_ref, lives_ref, parts_ref, out_ref):
    out_ref[...] = jnp.zeros(out_ref.shape, BF16)
    for h, block, part, live, slot in halves_of(lambda b: plan_ref[b], lambda b: lives_ref[b]):

        @pl.when(live)
        def _():
            total = parts_ref[0, slot].astype(F32)
            for k in range(1, YY):
                total = total + parts_ref[k, slot].astype(F32)
            out_ref[2 * plan_ref[block] + part] = total.astype(BF16)


def project_kernel(rows_ref, own_ref, other_ref, out_ref, weights, arrived):
    share = own_ref.shape[1]
    copies = []
    for k in range(4):
        source = (own_ref, other_ref)[k % 2]
        copies.append(
            pltpu.make_async_copy(source.at[k // 2], weights.at[pl.ds(k * share, share)], arrived.at[k])
        )
        copies[-1].start()
    rows = rows_ref[...]
    have = 0
    for low in range(0, 4 * share, WIDE):
        high = min(low + WIDE, 4 * share)
        while have < high:
            copies[have // share].wait()
            have += share
        out_ref[:, low:high] = lax.dot_general(
            rows, weights[low:high], (((1,), (1,)), ((), ())), preferred_element_type=F32
        )


def project(rows, own, other):
    count, features = rows.shape
    columns = 4 * own.shape[1]
    return pl.pallas_call(
        project_kernel,
        out_shape=jax.ShapeDtypeStruct((count, columns), F32),
        in_specs=[pl.BlockSpec(memory_space=pltpu.VMEM)] + [pl.BlockSpec(memory_space=pl.ANY)] * 2,
        out_specs=pl.BlockSpec(memory_space=pltpu.VMEM),
        scratch_shapes=[pltpu.VMEM((columns, features), BF16), pltpu.SemaphoreType.DMA((4,))],
        compiler_params=pltpu.CompilerParams(vmem_limit_bytes=32 << 20),
        cost_estimate=pl.CostEstimate(
            flops=2 * count * columns * features, bytes_accessed=2 * columns * features, transcendentals=0
        ),
    )(rows, own, other)


def local_call(kernel, scalars, shape):
    return pl.pallas_call(
        kernel,
        out_shape=jax.ShapeDtypeStruct(shape, BF16),
        in_specs=[pl.BlockSpec(memory_space=pltpu.SMEM)] * scalars + [pl.BlockSpec(memory_space=pltpu.VMEM)],
        out_specs=pl.BlockSpec(memory_space=pltpu.VMEM),
        compiler_params=pltpu.CompilerParams(vmem_limit_bytes=16 << 20),
    )


def exchange(array, axis):
    return lax.all_to_all(array, axis, 0, 0, tiled=False)


def swap(array, axis):
    return lax.ppermute(array, axis, [(0, 1), (1, 0)])


def spread(array, copies):
    return jnp.broadcast_to(array[None], (copies,) + array.shape)


def block_rows(slots, gathered, plan, lives, own, other, down):
    features, hidden = own.shape[2], 2 * down[0].shape[0]
    per = slots * 8
    place = (lax.axis_index("y") * 16 + lax.axis_index("c") * 8).reshape(1)
    packed = local_call(functools.partial(pack_kernel, slots), 3, (YY, slots, 8, features))(plan, lives, place, gathered)
    rows = exchange(packed.reshape(YY, per, features), "y").reshape(YY * per, features)

    partial = project(rows, own, other)
    along_x = jnp.sum(exchange(partial.reshape(XX, per, 2 * hidden), "x"), axis=0)
    across = swap(along_x.astype(BF16), "zh").astype(F32)
    down = jnp.concatenate(down, axis=0)
    summed = along_x + across
    act = (jax.nn.silu(summed[:, :hidden]) * summed[:, hidden:]).astype(BF16)
    act = exchange(spread(act, XX), "x").reshape(XX * per, hidden)

    ours = jnp.dot(act, down, preferred_element_type=F32).astype(BF16)
    parts = exchange(ours.reshape(YY, per, -1), "y").reshape(YY, slots, 8, -1)
    return local_call(place_kernel, 2, (ZL, 8, down.shape[1]))(plan, lives, parts)


def body(tokens, plan, lives, weights, down):
    gathered = exchange(spread(tokens, ZL), "zl")
    weights = weights.transpose(1, 2, 0)
    other = swap(weights, "c")
    down = (down, swap(down, "c"))
    if len(SIZES) == 1:
        placed = block_rows(SIZES[0], gathered, plan, lives, weights, other, down)
    else:
        count = jnp.sum((plan >= 0) * (1 + (lives > HALF)))
        which = sum((count > n).astype(jnp.int32) for n in SIZES[:-1])
        placed = lax.switch(
            which, [functools.partial(block_rows, n) for n in SIZES], gathered, plan, lives, weights, other, down
        )
    sums = exchange(placed, "zl")
    total = sums[0].astype(F32)
    for k in range(1, ZL):
        total = total + sums[k].astype(F32)
    return total.astype(BF16)


def solution(mesh):
    fine = Mesh(mesh.devices.reshape(ZL, YY, CC, XX, ZH), ("zl", "y", "c", "x", "zh"))
    dp, fsdp = ("zl", "y", "c"), ("x", "zh")
    return jax.shard_map(
        body,
        mesh=fine,
        in_specs=(P(dp, fsdp), P(), P(), P(fsdp, None, dp), P(dp, fsdp)),
        out_specs=P(dp, fsdp),
        check_vma=False,
    )
```

```python
import functools

import jax
import jax.numpy as jnp
from jax import lax
from jax.experimental import pallas as pl
from jax.experimental.pallas import tpu as pltpu
from jax.sharding import Mesh
from jax.sharding import PartitionSpec as P

BLK = 128
HALF = 64
ZL, YY, CC, XX, ZH = 8, 4, 2, 4, 2
HIDE = 40_000_000_000
WIDE = 256
SIZES = (2, 3, 4, 5, 6, 8)
BF16, F32 = jnp.bfloat16, jnp.float32


def halves_of(plan, lives):
    slot = jnp.int32(0)
    for h in range(ZL):
        block, part = h // 2, h % 2
        live = (plan(block) >= 0) & (lives(block) > HALF * part)
        yield h, block, part, live, slot
        slot = slot + live.astype(jnp.int32)


def size_kernel(plan_ref, lives_ref, out_ref):
    count = jnp.int32(0)
    for h, block, part, live, slot in halves_of(lambda b: plan_ref[b], lambda b: lives_ref[b]):
        count = slot + live.astype(jnp.int32)
    which = jnp.int32(0)
    for n in SIZES[:-1]:
        which = which + (count > n).astype(jnp.int32)
    out_ref[0] = which


def pick_size(plan, lives):
    return pl.pallas_call(
        size_kernel,
        out_shape=jax.ShapeDtypeStruct((1,), jnp.int32),
        in_specs=[pl.BlockSpec(memory_space=pltpu.SMEM)] * 2,
        out_specs=pl.BlockSpec(memory_space=pltpu.SMEM),
        compiler_params=pltpu.CompilerParams(vmem_limit_bytes=1 << 20),
        cost_estimate=pl.CostEstimate(flops=HIDE, bytes_accessed=0, transcendentals=0),
    )(plan, lives)[0]


def pack_kernel(slots, plan_ref, lives_ref, place_ref, rows_ref, out_ref):
    row = lax.broadcasted_iota(jnp.int32, rows_ref.shape[1:], 0) + place_ref[0]
    count = jnp.int32(0)
    for h, block, part, live, slot in halves_of(lambda b: plan_ref[b], lambda b: lives_ref[b]):
        count = slot + live.astype(jnp.int32)

        @pl.when(live)
        def _():
            kept = row + HALF * part < lives_ref[block]
            rows = jnp.where(kept, rows_ref[h].astype(F32), 0.0).astype(BF16)
            for copy in range(YY):
                out_ref[copy, slot] = rows

    for s in range(slots):

        @pl.when(s >= count)
        def _():
            for copy in range(YY):
                out_ref[copy, s] = jnp.zeros(out_ref.shape[2:], BF16)


def place_kernel(plan_ref, lives_ref, parts_ref, out_ref):
    out_ref[...] = jnp.zeros(out_ref.shape, BF16)
    for h, block, part, live, slot in halves_of(lambda b: plan_ref[b], lambda b: lives_ref[b]):

        @pl.when(live)
        def _():
            total = parts_ref[0, slot].astype(F32)
            for k in range(1, YY):
                total = total + parts_ref[k, slot].astype(F32)
            out_ref[2 * plan_ref[block] + part] = total.astype(BF16)


def project_kernel(rows_ref, own_ref, other_ref, out_ref, weights, arrived):
    share = own_ref.shape[1]
    copies = []
    for k in range(4):
        source = (own_ref, other_ref)[k % 2]
        copies.append(
            pltpu.make_async_copy(source.at[k // 2], weights.at[pl.ds(k * share, share)], arrived.at[k])
        )
        copies[-1].start()
    rows = rows_ref[...]
    have = 0
    for low in range(0, 4 * share, WIDE):
        high = min(low + WIDE, 4 * share)
        while have < high:
            copies[have // share].wait()
            have += share
        out_ref[:, low:high] = lax.dot_general(
            rows, weights[low:high], (((1,), (1,)), ((), ())), preferred_element_type=F32
        )


def project(rows, own, other):
    count, features = rows.shape
    columns = 4 * own.shape[1]
    return pl.pallas_call(
        project_kernel,
        out_shape=jax.ShapeDtypeStruct((count, columns), F32),
        in_specs=[pl.BlockSpec(memory_space=pltpu.VMEM)] + [pl.BlockSpec(memory_space=pl.ANY)] * 2,
        out_specs=pl.BlockSpec(memory_space=pltpu.VMEM),
        scratch_shapes=[pltpu.VMEM((columns, features), BF16), pltpu.SemaphoreType.DMA((4,))],
        compiler_params=pltpu.CompilerParams(vmem_limit_bytes=32 << 20),
        cost_estimate=pl.CostEstimate(
            flops=2 * count * columns * features, bytes_accessed=2 * columns * features, transcendentals=0
        ),
    )(rows, own, other)


def local_call(kernel, scalars, shape):
    return pl.pallas_call(
        kernel,
        out_shape=jax.ShapeDtypeStruct(shape, BF16),
        in_specs=[pl.BlockSpec(memory_space=pltpu.SMEM)] * scalars + [pl.BlockSpec(memory_space=pltpu.VMEM)],
        out_specs=pl.BlockSpec(memory_space=pltpu.VMEM),
        compiler_params=pltpu.CompilerParams(vmem_limit_bytes=16 << 20),
    )


def exchange(array, axis):
    return lax.all_to_all(array, axis, 0, 0, tiled=False)


def swap(array, axis):
    return lax.ppermute(array, axis, [(0, 1), (1, 0)])


def spread(array, copies):
    return jnp.broadcast_to(array[None], (copies,) + array.shape)


def block_rows(slots, gathered, plan, lives, own, other, down):
    features, hidden = own.shape[2], 2 * down[0].shape[0]
    per = slots * 8
    place = (lax.axis_index("y") * 16 + lax.axis_index("c") * 8).reshape(1)
    packed = local_call(functools.partial(pack_kernel, slots), 3, (YY, slots, 8, features))(plan, lives, place, gathered)
    rows = exchange(packed.reshape(YY, per, features), "y").reshape(YY * per, features)

    partial = project(rows, own, other)
    along_x = jnp.sum(exchange(partial.reshape(XX, per, 2 * hidden), "x"), axis=0)
    across = swap(along_x.astype(BF16), "zh").astype(F32)
    down = jnp.concatenate(down, axis=0)
    summed = along_x + across
    act = (jax.nn.silu(summed[:, :hidden]) * summed[:, hidden:]).astype(BF16)
    act = exchange(spread(act, XX), "x").reshape(XX * per, hidden)

    ours = jnp.dot(act, down, preferred_element_type=F32).astype(BF16)
    parts = exchange(ours.reshape(YY, per, -1), "y").reshape(YY, slots, 8, -1)
    return local_call(place_kernel, 2, (ZL, 8, down.shape[1]))(plan, lives, parts)


def body(tokens, plan, lives, weights, down):
    gathered = exchange(spread(tokens, ZL), "zl")
    weights = weights.transpose(1, 2, 0)
    other = swap(weights, "c")
    down = (down, swap(down, "c"))
    placed = lax.switch(
        pick_size(plan, lives),
        [functools.partial(block_rows, n) for n in SIZES],
        gathered, plan, lives, weights, other, down,
    )
    sums = exchange(placed, "zl")
    total = sums[0].astype(F32)
    for k in range(1, ZL):
        total = total + sums[k].astype(F32)
    return total.astype(BF16)


def solution(mesh):
    fine = Mesh(mesh.devices.reshape(ZL, YY, CC, XX, ZH), ("zl", "y", "c", "x", "zh"))
    dp, fsdp = ("zl", "y", "c"), ("x", "zh")
    return jax.shard_map(
        body,
        mesh=fine,
        in_specs=(P(dp, fsdp), P(), P(), P(fsdp, None, dp), P(dp, fsdp)),
        out_specs=P(dp, fsdp),
        check_vma=False,
    )
```

```python
import functools

import jax
import jax.numpy as jnp
from jax import lax
from jax.experimental import pallas as pl
from jax.experimental.pallas import tpu as pltpu
from jax.sharding import Mesh
from jax.sharding import PartitionSpec as P

BLK = 128
HALF = 64
ZL, YY, CC, XX, ZH = 8, 4, 2, 4, 2
HIDE = 40_000_000_000
GATHER = (5, 6)
WIDE = 256
SIZES = (2, 3, 4, 5, 6, 8)
BF16, F32 = jnp.bfloat16, jnp.float32


def halves_of(plan, lives):
    slot = jnp.int32(0)
    for h in range(ZL):
        block, part = h // 2, h % 2
        live = (plan(block) >= 0) & (lives(block) > HALF * part)
        yield h, block, part, live, slot
        slot = slot + live.astype(jnp.int32)


def size_kernel(plan_ref, lives_ref, out_ref):
    count = jnp.int32(0)
    for h, block, part, live, slot in halves_of(lambda b: plan_ref[b], lambda b: lives_ref[b]):
        count = slot + live.astype(jnp.int32)
    which = jnp.int32(0)
    for n in SIZES[:-1]:
        which = which + (count > n).astype(jnp.int32)
    out_ref[0] = which


def pick_size(plan, lives):
    return pl.pallas_call(
        size_kernel,
        out_shape=jax.ShapeDtypeStruct((1,), jnp.int32),
        in_specs=[pl.BlockSpec(memory_space=pltpu.SMEM)] * 2,
        out_specs=pl.BlockSpec(memory_space=pltpu.SMEM),
        compiler_params=pltpu.CompilerParams(vmem_limit_bytes=1 << 20),
        cost_estimate=pl.CostEstimate(flops=HIDE, bytes_accessed=0, transcendentals=0),
    )(plan, lives)[0]


def pack_kernel(slots, plan_ref, lives_ref, place_ref, rows_ref, out_ref):
    row = lax.broadcasted_iota(jnp.int32, rows_ref.shape[1:], 0) + place_ref[0]
    count = jnp.int32(0)
    for h, block, part, live, slot in halves_of(lambda b: plan_ref[b], lambda b: lives_ref[b]):
        count = slot + live.astype(jnp.int32)

        @pl.when(live)
        def _():
            kept = row + HALF * part < lives_ref[block]
            rows = jnp.where(kept, rows_ref[h].astype(F32), 0.0).astype(BF16)
            for copy in range(out_ref.shape[0]):
                out_ref[copy, slot] = rows

    for s in range(slots):

        @pl.when(s >= count)
        def _():
            for copy in range(out_ref.shape[0]):
                out_ref[copy, s] = jnp.zeros(out_ref.shape[2:], BF16)


def place_kernel(plan_ref, lives_ref, parts_ref, out_ref):
    out_ref[...] = jnp.zeros(out_ref.shape, BF16)
    for h, block, part, live, slot in halves_of(lambda b: plan_ref[b], lambda b: lives_ref[b]):

        @pl.when(live)
        def _():
            total = parts_ref[0, slot].astype(F32)
            for k in range(1, YY):
                total = total + parts_ref[k, slot].astype(F32)
            out_ref[2 * plan_ref[block] + part] = total.astype(BF16)


def project_kernel(rows_ref, own_ref, other_ref, out_ref, weights, arrived):
    share = own_ref.shape[1]
    copies = []
    for k in range(4):
        source = (own_ref, other_ref)[k % 2]
        copies.append(
            pltpu.make_async_copy(source.at[k // 2], weights.at[pl.ds(k * share, share)], arrived.at[k])
        )
        copies[-1].start()
    rows = rows_ref[...]
    have = 0
    for low in range(0, 4 * share, WIDE):
        high = min(low + WIDE, 4 * share)
        while have < high:
            copies[have // share].wait()
            have += share
        out_ref[:, low:high] = lax.dot_general(
            rows, weights[low:high], (((1,), (1,)), ((), ())), preferred_element_type=F32
        )


def project(rows, own, other):
    count, features = rows.shape
    columns = 4 * own.shape[1]
    return pl.pallas_call(
        project_kernel,
        out_shape=jax.ShapeDtypeStruct((count, columns), F32),
        in_specs=[pl.BlockSpec(memory_space=pltpu.VMEM)] + [pl.BlockSpec(memory_space=pl.ANY)] * 2,
        out_specs=pl.BlockSpec(memory_space=pltpu.VMEM),
        scratch_shapes=[pltpu.VMEM((columns, features), BF16), pltpu.SemaphoreType.DMA((4,))],
        compiler_params=pltpu.CompilerParams(vmem_limit_bytes=32 << 20),
        cost_estimate=pl.CostEstimate(
            flops=2 * count * columns * features, bytes_accessed=2 * columns * features, transcendentals=0
        ),
    )(rows, own, other)


def local_call(kernel, scalars, shape):
    return pl.pallas_call(
        kernel,
        out_shape=jax.ShapeDtypeStruct(shape, BF16),
        in_specs=[pl.BlockSpec(memory_space=pltpu.SMEM)] * scalars + [pl.BlockSpec(memory_space=pltpu.VMEM)],
        out_specs=pl.BlockSpec(memory_space=pltpu.VMEM),
        compiler_params=pltpu.CompilerParams(vmem_limit_bytes=16 << 20),
    )


def exchange(array, axis):
    return lax.all_to_all(array, axis, 0, 0, tiled=False)


def swap(array, axis):
    return lax.ppermute(array, axis, [(0, 1), (1, 0)])


def spread(array, copies):
    return jnp.broadcast_to(array[None], (copies,) + array.shape)


def block_rows(slots, gathered, plan, lives, own, other, down):
    features, hidden = own.shape[2], 2 * down[0].shape[0]
    per = slots * 8
    place = (lax.axis_index("y") * 16 + lax.axis_index("c") * 8).reshape(1)
    copies = 1 if slots in GATHER else YY
    packed = local_call(functools.partial(pack_kernel, slots), 3, (copies, slots, 8, features))(plan, lives, place, gathered)
    if copies == 1:
        rows = lax.all_gather(packed.reshape(per, features), "y", axis=0, tiled=True)
    else:
        rows = exchange(packed.reshape(YY, per, features), "y").reshape(YY * per, features)

    partial = project(rows, own, other)
    along_x = jnp.sum(exchange(partial.reshape(XX, per, 2 * hidden), "x"), axis=0)
    across = swap(along_x.astype(BF16), "zh").astype(F32)
    down = jnp.concatenate(down, axis=0)
    summed = along_x + across
    act = (jax.nn.silu(summed[:, :hidden]) * summed[:, hidden:]).astype(BF16)
    act = exchange(spread(act, XX), "x").reshape(XX * per, hidden)

    ours = jnp.dot(act, down, preferred_element_type=F32).astype(BF16)
    parts = exchange(ours.reshape(YY, per, -1), "y").reshape(YY, slots, 8, -1)
    return local_call(place_kernel, 2, (ZL, 8, down.shape[1]))(plan, lives, parts)


def body(tokens, plan, lives, weights, down):
    gathered = exchange(spread(tokens, ZL), "zl")
    weights = weights.transpose(1, 2, 0)
    other = swap(weights, "c")
    down = (down, swap(down, "c"))
    placed = lax.switch(
        pick_size(plan, lives),
        [functools.partial(block_rows, n) for n in SIZES],
        gathered, plan, lives, weights, other, down,
    )
    sums = exchange(placed, "zl")
    total = sums[0].astype(F32)
    for k in range(1, ZL):
        total = total + sums[k].astype(F32)
    return total.astype(BF16)


def solution(mesh):
    fine = Mesh(mesh.devices.reshape(ZL, YY, CC, XX, ZH), ("zl", "y", "c", "x", "zh"))
    dp, fsdp = ("zl", "y", "c"), ("x", "zh")
    return jax.shard_map(
        body,
        mesh=fine,
        in_specs=(P(dp, fsdp), P(), P(), P(fsdp, None, dp), P(dp, fsdp)),
        out_specs=P(dp, fsdp),
        check_vma=False,
    )
```

```python
import functools

import jax
import jax.numpy as jnp
from jax import lax
from jax.experimental import pallas as pl
from jax.experimental.pallas import tpu as pltpu
from jax.sharding import Mesh
from jax.sharding import PartitionSpec as P

BLK = 128
HALF = 64
ZL, YY, CC, XX, ZH = 8, 4, 2, 4, 2
HIDE = 40_000_000_000
GATHER = (5, 6)
WIDE = 256
SIZES = (1, 2, 3, 4, 5, 6, 7, 8)
BF16, F32 = jnp.bfloat16, jnp.float32


def halves_of(plan, lives):
    slot = jnp.int32(0)
    for h in range(ZL):
        block, part = h // 2, h % 2
        live = (plan(block) >= 0) & (lives(block) > HALF * part)
        yield h, block, part, live, slot
        slot = slot + live.astype(jnp.int32)


def size_kernel(plan_ref, lives_ref, out_ref):
    count = jnp.int32(0)
    for h, block, part, live, slot in halves_of(lambda b: plan_ref[b], lambda b: lives_ref[b]):
        count = slot + live.astype(jnp.int32)
    which = jnp.int32(0)
    for n in SIZES[:-1]:
        which = which + (count > n).astype(jnp.int32)
    out_ref[0] = which


def pick_size(plan, lives):
    return pl.pallas_call(
        size_kernel,
        out_shape=jax.ShapeDtypeStruct((1,), jnp.int32),
        in_specs=[pl.BlockSpec(memory_space=pltpu.SMEM)] * 2,
        out_specs=pl.BlockSpec(memory_space=pltpu.SMEM),
        compiler_params=pltpu.CompilerParams(vmem_limit_bytes=1 << 20),
        cost_estimate=pl.CostEstimate(flops=HIDE, bytes_accessed=0, transcendentals=0),
    )(plan, lives)[0]


def pack_kernel(slots, plan_ref, lives_ref, place_ref, rows_ref, out_ref):
    row = lax.broadcasted_iota(jnp.int32, rows_ref.shape[1:], 0) + place_ref[0]
    count = jnp.int32(0)
    for h, block, part, live, slot in halves_of(lambda b: plan_ref[b], lambda b: lives_ref[b]):
        count = slot + live.astype(jnp.int32)

        @pl.when(live)
        def _():
            kept = row + HALF * part < lives_ref[block]
            rows = jnp.where(kept, rows_ref[h].astype(F32), 0.0).astype(BF16)
            for copy in range(out_ref.shape[0]):
                out_ref[copy, slot] = rows

    for s in range(slots):

        @pl.when(s >= count)
        def _():
            for copy in range(out_ref.shape[0]):
                out_ref[copy, s] = jnp.zeros(out_ref.shape[2:], BF16)


def place_kernel(plan_ref, lives_ref, parts_ref, out_ref):
    out_ref[...] = jnp.zeros(out_ref.shape, BF16)
    for h, block, part, live, slot in halves_of(lambda b: plan_ref[b], lambda b: lives_ref[b]):

        @pl.when(live)
        def _():
            total = parts_ref[0, slot].astype(F32)
            for k in range(1, YY):
                total = total + parts_ref[k, slot].astype(F32)
            out_ref[2 * plan_ref[block] + part] = total.astype(BF16)


def project_kernel(rows_ref, own_ref, other_ref, out_ref, weights, arrived):
    share = own_ref.shape[1]
    copies = []
    for k in range(4):
        source = (own_ref, other_ref)[k % 2]
        copies.append(
            pltpu.make_async_copy(source.at[k // 2], weights.at[pl.ds(k * share, share)], arrived.at[k])
        )
        copies[-1].start()
    rows = rows_ref[...]
    have = 0
    for low in range(0, 4 * share, WIDE):
        high = min(low + WIDE, 4 * share)
        while have < high:
            copies[have // share].wait()
            have += share
        out_ref[:, low:high] = lax.dot_general(
            rows, weights[low:high], (((1,), (1,)), ((), ())), preferred_element_type=F32
        )


def project(rows, own, other):
    count, features = rows.shape
    columns = 4 * own.shape[1]
    return pl.pallas_call(
        project_kernel,
        out_shape=jax.ShapeDtypeStruct((count, columns), F32),
        in_specs=[pl.BlockSpec(memory_space=pltpu.VMEM)] + [pl.BlockSpec(memory_space=pl.ANY)] * 2,
        out_specs=pl.BlockSpec(memory_space=pltpu.VMEM),
        scratch_shapes=[pltpu.VMEM((columns, features), BF16), pltpu.SemaphoreType.DMA((4,))],
        compiler_params=pltpu.CompilerParams(vmem_limit_bytes=32 << 20),
        cost_estimate=pl.CostEstimate(
            flops=2 * count * columns * features, bytes_accessed=2 * columns * features, transcendentals=0
        ),
    )(rows, own, other)


def local_call(kernel, scalars, shape):
    return pl.pallas_call(
        kernel,
        out_shape=jax.ShapeDtypeStruct(shape, BF16),
        in_specs=[pl.BlockSpec(memory_space=pltpu.SMEM)] * scalars + [pl.BlockSpec(memory_space=pltpu.VMEM)],
        out_specs=pl.BlockSpec(memory_space=pltpu.VMEM),
        compiler_params=pltpu.CompilerParams(vmem_limit_bytes=16 << 20),
    )


def exchange(array, axis):
    return lax.all_to_all(array, axis, 0, 0, tiled=False)


def swap(array, axis):
    return lax.ppermute(array, axis, [(0, 1), (1, 0)])


def spread(array, copies):
    return jnp.broadcast_to(array[None], (copies,) + array.shape)


def block_rows(slots, gathered, plan, lives, own, other, down):
    features, hidden = own.shape[2], 2 * down[0].shape[0]
    per = slots * 8
    place = (lax.axis_index("y") * 16 + lax.axis_index("c") * 8).reshape(1)
    copies = 1 if slots in GATHER else YY
    packed = local_call(functools.partial(pack_kernel, slots), 3, (copies, slots, 8, features))(plan, lives, place, gathered)
    if copies == 1:
        rows = lax.all_gather(packed.reshape(per, features), "y", axis=0, tiled=True)
    else:
        rows = exchange(packed.reshape(YY, per, features), "y").reshape(YY * per, features)

    partial = project(rows, own, other)
    along_x = jnp.sum(exchange(partial.reshape(XX, per, 2 * hidden), "x"), axis=0)
    across = swap(along_x.astype(BF16), "zh").astype(F32)
    down = jnp.concatenate(down, axis=0)
    summed = along_x + across
    act = (jax.nn.silu(summed[:, :hidden]) * summed[:, hidden:]).astype(BF16)
    act = exchange(spread(act, XX), "x").reshape(XX * per, hidden)

    ours = jnp.dot(act, down, preferred_element_type=F32).astype(BF16)
    parts = exchange(ours.reshape(YY, per, -1), "y").reshape(YY, slots, 8, -1)
    return local_call(place_kernel, 2, (ZL, 8, down.shape[1]))(plan, lives, parts)


def body(tokens, plan, lives, weights, down):
    gathered = exchange(spread(tokens, ZL), "zl")
    weights = weights.transpose(1, 2, 0)
    other = swap(weights, "c")
    down = (down, swap(down, "c"))
    placed = lax.switch(
        pick_size(plan, lives),
        [functools.partial(block_rows, n) for n in SIZES],
        gathered, plan, lives, weights, other, down,
    )
    sums = exchange(placed, "zl")
    total = sums[0].astype(F32)
    for k in range(1, ZL):
        total = total + sums[k].astype(F32)
    return total.astype(BF16)


def solution(mesh):
    fine = Mesh(mesh.devices.reshape(ZL, YY, CC, XX, ZH), ("zl", "y", "c", "x", "zh"))
    dp, fsdp = ("zl", "y", "c"), ("x", "zh")
    return jax.shard_map(
        body,
        mesh=fine,
        in_specs=(P(dp, fsdp), P(), P(), P(fsdp, None, dp), P(dp, fsdp)),
        out_specs=P(dp, fsdp),
        check_vma=False,
    )
```
